256 devices in a mesh: group: 4 (over x), member: 64 (over y, z, core).
Axes of the slice: x: 4, y: 4, z: 8, core: 2. Of those that a mesh axis runs over, the one named last changes fastest.
Arguments:
- embeddings: bfloat16 [49152, 1024], P(('group', 'member'))
- first_size: int32 [4], P('group'), may hold values from 1536 to 10751
Outputs:
- best_match: float32 [49152], P(('group', 'member'))
The draws below stay inside these ranges and needn't reach their ends.
All inputs are finite; a program needn't handle non-finite values.
Results may differ from the reference program's by a relative error of at most 0.0045.
Values may be sent and summed in bfloat16 or wider, within the bound.
No kernel may reach another device: no remote copies, remote signals or barrier semaphores. Data moves between devices by JAX's collectives and lax.ppermute only.
A program may use at most 64 MiB of HBM per device.

```python
import math
import jax
import jax.numpy as jnp
from jax import lax

D = 1024
GROUPS = 4
ROWS_GROUP = 12288
ROWS = 49152


def draw_embeddings(key, part):
    key = jax.random.fold_in(key, 11)
    keys = jax.random.split(key, 4)
    base = jax.random.normal(keys[0], (ROWS, D), jnp.float32)
    scale = jnp.exp(jax.random.uniform(keys[3], (ROWS, 1), jnp.float32, 0.0, 2.3))
    offset = jnp.arange(ROWS, dtype=jnp.int32) // ROWS_GROUP * ROWS_GROUP
    source = offset + jax.random.randint(keys[1], (ROWS,), 0, ROWS_GROUP)
    strength = jax.random.uniform(keys[2], (ROWS, 1), jnp.float32, 0.0, 0.95)
    mixed = strength * base[source] + jnp.sqrt(1.0 - strength * strength) * base
    return (mixed * scale).astype(jnp.bfloat16)


def touch_ends(result, key, low, largest):
    longest = result.shape.index(max(result.shape))
    spots = []
    for shift in (0, 1):
        where = [jax.random.randint(jax.random.fold_in(key, axis), (), 0, length) for axis, length in enumerate(result.shape)]
        where[longest] = (where[longest] + shift) % result.shape[longest]
        spots.append(tuple(where))
    return result.at[spots[0]].set(low).at[spots[1]].set(largest)


def setup_inputs(seed: int = 0) -> dict:
    key_of = jax.random.split(jax.random.key(seed), 3)
    return {
        "embeddings": draw_embeddings(jax.random.fold_in(key_of[2], 71), 0),
        "first_size": touch_ends(jax.random.randint(key_of[1], (GROUPS,), ROWS_GROUP // 8, ROWS_GROUP - ROWS_GROUP // 8), jax.random.fold_in(key_of[1], 1), ROWS_GROUP // 8, (ROWS_GROUP - ROWS_GROUP // 8) - 1).astype(jnp.int32),
    }


def normalize(rows):
    values = rows.astype(jnp.float32)
    return (values * lax.rsqrt(lax.optimization_barrier(jnp.sum(values * values, axis=1, keepdims=True)) + 1e-06)).astype(jnp.bfloat16)

def reference(embeddings, first_size):
    block = math.gcd(ROWS_GROUP, 512)
    results = []
    for group_id in range(GROUPS):
        unit = normalize(embeddings[group_id * ROWS_GROUP:(group_id + 1) * ROWS_GROUP])
        split = first_size[group_id]
        index = jnp.arange(ROWS_GROUP, dtype=jnp.int32)
        cluster = index >= split

        def one_block(start):
            rows = lax.dynamic_slice_in_dim(unit, start, block, 0)
            row_index = start + jnp.arange(block, dtype=jnp.int32)
            scores = jnp.dot(rows, unit.T, preferred_element_type=jnp.float32)
            keep = (index[None, :] < row_index[:, None]) & (cluster[None, :] == (row_index >= split)[:, None])
            return lax.optimization_barrier(jnp.max(jnp.where(keep, scores, -1.0), axis=1))
        starts = jnp.arange(ROWS_GROUP // block, dtype=jnp.int32) * block
        results.append(lax.map(one_block, starts).reshape(ROWS_GROUP))
    return jnp.concatenate(results).astype(jnp.float32)
```

```python
import jax
import jax.numpy as jnp
from jax import lax
from jax.experimental import pallas as pl
from jax.experimental.pallas import tpu as pltpu
from jax.sharding import PartitionSpec as P

Y, Z, CORES = 4, 8, 2
ROWS = 192
HALF = ROWS // 2
CHIP = ROWS * CORES
WIDE = Y * CHIP
D = 1024
NONE = -2.0


def device(y, z, core):
    return ((y % Y) * Z + z % Z) * CORES + core % CORES


def move(value, dy, dz, dcore=0):
    pairs = [
        (device(y, z, core), device(y + dy, z + dz, core + dcore))
        for y in range(Y)
        for z in range(Z)
        for core in range(CORES)
    ]
    return lax.ppermute(value, "member", pairs)


def normalize_kernel(rows_ref, low_ref, high_ref):
    values = rows_ref[...].astype(jnp.float32)
    unit = (values * lax.rsqrt(jnp.sum(values * values, axis=1, keepdims=True) + 1e-06)).astype(
        jnp.bfloat16
    )
    low_ref[...] = unit[:HALF]
    high_ref[...] = unit[HALF:]


def normalize(rows):
    half = jax.ShapeDtypeStruct((HALF, D), jnp.bfloat16)
    return pl.pallas_call(
        normalize_kernel,
        out_shape=(half, half),
        cost_estimate=pl.CostEstimate(flops=4 * ROWS * D, bytes_accessed=4 * ROWS * D, transcendentals=ROWS),
        name="normalize",
    )(rows)


def match_kernel(starts_ref, lo_ref, hi_ref, best_ref, right_ref, *rest):
    *piece_refs, out_ref = rest
    tile = 256
    for n in range(WIDE // tile):
        lanes = slice(n * tile, (n + 1) * tile)
        right = right_ref[lanes, :]
        lo = lo_ref[:, lanes]
        hi = hi_ref[:, lanes]
        best = best_ref[:, lanes]
        for i, piece_ref in enumerate(piece_refs):
            scores = lax.dot_general(
                piece_ref[...], right, (((1,), (1,)), ((), ())), preferred_element_type=jnp.float32
            )
            index = starts_ref[i] + lax.broadcasted_iota(jnp.int32, scores.shape, 0)
            scores = jnp.where((index >= lo) & (index < hi), scores, NONE)
            best = jnp.maximum(best, jnp.max(scores.reshape(-1, 8, tile), axis=0))
        out_ref[:, lanes] = best


def match(starts, lo, hi, best, right, pieces):
    vmem = pl.BlockSpec(memory_space=pltpu.VMEM)
    rows = sum(piece.shape[0] for piece in pieces)
    return pl.pallas_call(
        match_kernel,
        out_shape=jax.ShapeDtypeStruct((8, WIDE), jnp.float32),
        in_specs=[pl.BlockSpec(memory_space=pltpu.SMEM)] + [vmem] * (4 + len(pieces)),
        out_specs=vmem,
        cost_estimate=pl.CostEstimate(
            flops=2 * rows * WIDE * D, bytes_accessed=2 * D * (rows + WIDE), transcendentals=0
        ),
        compiler_params=pltpu.CompilerParams(vmem_limit_bytes=24 * 1024 * 1024),
        name="match",
    )(starts, lo, hi, best, right, *pieces)


def shards(embeddings, first_size):
    member = lax.axis_index("member")
    core = member % CORES
    z = member // CORES % Z
    y = member // (CORES * Z)
    split = first_size[0]

    unit = normalize(embeddings)

    def start(dy, dz, half, dcore=0):
        return device(y + dy, z + dz, core + dcore) * ROWS + half * HALF

    row_index = jnp.concatenate(
        [
            start(dy, 0, 0, dcore) + jnp.arange(ROWS, dtype=jnp.int32)
            for dcore in (0, 1)
            for dy in (0, -1, 1, 2)
        ]
    )[None]
    lo = jnp.where(row_index >= split, split, 0)

    up, down = [unit], [unit]
    for _ in range(3):
        up.append([move(half, 0, 1) for half in up[-1]])
        down.append([move(half, 0, -1) for half in down[-1]])
    far = [move(up[3][0], 0, 1), move(down[3][1], 0, -1)]

    above = [move(half, 1, 0) for half in unit]
    below = [move(half, -1, 0) for half in unit]
    across = [move(above[0], 1, 0), move(below[1], -1, 0)]
    mine = jnp.concatenate(list(unit) + above + below + across)
    right = jnp.concatenate([mine, move(mine, 0, 0, 1)])

    best = jnp.full((8, WIDE), NONE, jnp.float32)
    best = match(jnp.stack([start(0, 0, h) for h in (0, 1)]), lo, row_index, best, right, unit)
    for k in (1, 2, 3):
        starts = jnp.stack([start(0, d, h) for d in (-k, k) for h in (0, 1)])
        best = match(starts, lo, row_index, best, right, up[k] + down[k])
    best = match(jnp.stack([start(0, 4, h) for h in (0, 1)]), lo, row_index, best, right, far)

    best = jnp.max(best, axis=0).reshape(CORES, Y, ROWS)
    best = jnp.maximum(best[0], move(best[1], 0, 0, 1))
    best = jnp.maximum(
        jnp.maximum(best[0], move(best[1], -1, 0)),
        jnp.maximum(move(best[2], 1, 0), move(best[3], 2, 0)),
    )
    return jnp.maximum(best, -1.0)


def solution(mesh):
    placed = (P(("group", "member"), None), P("group"))
    return jax.shard_map(
        shards, mesh=mesh, in_specs=placed, out_specs=P(("group", "member")), check_vma=False
    )
```

```python
import functools

import jax
import jax.numpy as jnp
from jax import lax
from jax.experimental import pallas as pl
from jax.experimental.pallas import tpu as pltpu
from jax.sharding import PartitionSpec as P

Y, Z, CORES = 4, 8, 2
ROWS = 192
SEGMENTS = Y * CORES
WIDE = SEGMENTS * ROWS
TILE = 256
D = 1024
NONE = -2.0
VMEM = pl.BlockSpec(memory_space=pltpu.VMEM)
SMEM = pl.BlockSpec(memory_space=pltpu.SMEM)


def device(y, z, core):
    return ((y % Y) * Z + z % Z) * CORES + core % CORES


def permute(value, target):
    pairs = [
        (device(y, z, core), device(*target(y, z, core)))
        for y in range(Y)
        for z in range(Z)
        for core in range(CORES)
    ]
    return lax.ppermute(value, "member", pairs)


def along_y(value, dy):
    return permute(value, lambda y, z, core: (y + dy, z, core))


def along_z(value):
    return permute(value, lambda y, z, core: (y, z + (1, -1)[core], core))


def swap(value):
    return permute(value, lambda y, z, core: (y, z, core + 1))


def normalize_kernel(rows_ref, unit_ref):
    values = rows_ref[...].astype(jnp.float32)
    unit_ref[...] = (
        values * lax.rsqrt(jnp.sum(values * values, axis=1, keepdims=True) + 1e-06)
    ).astype(jnp.bfloat16)


def normalize(rows):
    return pl.pallas_call(
        normalize_kernel,
        out_shape=jax.ShapeDtypeStruct((ROWS, D), jnp.bfloat16),
        in_specs=[VMEM],
        out_specs=VMEM,
        cost_estimate=pl.CostEstimate(flops=4 * ROWS * D, bytes_accessed=4 * ROWS * D, transcendentals=ROWS),
        compiler_params=pltpu.CompilerParams(vmem_limit_bytes=8 * 1024 * 1024),
        name="normalize",
    )(rows)


def fold(starts_ref, lo_ref, hi_ref, best_ref, right_ref, left, out_ref):
    for n in range(WIDE // TILE):
        lanes = slice(n * TILE, (n + 1) * TILE)
        scores = lax.dot_general(
            left[...], right_ref[lanes, :], (((1,), (1,)), ((), ())), preferred_element_type=jnp.float32
        )
        lo, hi = lo_ref[:, lanes], hi_ref[:, lanes]
        best = None if best_ref is None else best_ref[:, lanes]
        for i in range(left.shape[0] // ROWS):
            index = starts_ref[i] + lax.broadcasted_iota(jnp.int32, (ROWS, TILE), 0)
            part = jnp.where((index >= lo) & (index < hi), scores[i * ROWS : (i + 1) * ROWS], NONE)
            part = jnp.max(part.reshape(-1, 8, TILE), axis=0)
            best = part if best is None else jnp.maximum(best, part)
        out_ref[:, lanes] = best


def stack(piece_refs, left):
    if len(piece_refs) == 1:
        return piece_refs[0]
    for i, piece_ref in enumerate(piece_refs):
        left[i * ROWS : (i + 1) * ROWS, :] = piece_ref[...]
    return left


def first_kernel(starts_ref, lo_ref, hi_ref, *refs):
    segments, pieces = refs[:SEGMENTS], refs[SEGMENTS:-3]
    right_ref, out_ref, left = refs[-3:]
    for i, segment in enumerate(segments):
        right_ref[i * ROWS : (i + 1) * ROWS, :] = segment[...]
    fold(starts_ref, lo_ref, hi_ref, None, right_ref, stack(pieces, left), out_ref)


def match_kernel(starts_ref, lo_ref, hi_ref, best_ref, right_ref, *refs):
    pieces, (out_ref, left) = refs[:-2], refs[-2:]
    fold(starts_ref, lo_ref, hi_ref, best_ref, right_ref, stack(pieces, left), out_ref)


def match(kernel, starts, lo, hi, others, pieces):
    rows = ROWS * len(pieces)
    best = jax.ShapeDtypeStruct((8, WIDE), jnp.float32)
    first = kernel is first_kernel
    return pl.pallas_call(
        kernel,
        out_shape=(jax.ShapeDtypeStruct((WIDE, D), jnp.bfloat16), best) if first else best,
        in_specs=[SMEM] + [VMEM] * (2 + len(others) + len(pieces)),
        out_specs=(VMEM, VMEM) if first else VMEM,
        scratch_shapes=[pltpu.VMEM((rows, D), jnp.bfloat16)],
        cost_estimate=pl.CostEstimate(
            flops=2 * rows * WIDE * D, bytes_accessed=2 * D * (rows + WIDE), transcendentals=0
        ),
        compiler_params=pltpu.CompilerParams(vmem_limit_bytes=16 * 1024 * 1024),
        name="match",
    )(jnp.stack(starts), lo, hi, *others, *pieces)


def shards(embeddings, first_size):
    member = lax.axis_index("member")
    core = member % CORES
    z = member // CORES % Z
    y = member // (CORES * Z)
    split = first_size[0]
    toward = 2 * core - 1

    unit = normalize(embeddings)

    def start(dy, dz, dcore):
        return device(y + dy, z + dz, core + dcore) * ROWS

    segment = jnp.arange(SEGMENTS, dtype=jnp.int32)[:, None]
    segment_dy = jnp.array([0, 3, 1, 2], jnp.int32)[segment % Y]
    row_index = start(segment_dy, 0, segment // Y) + jnp.arange(ROWS, dtype=jnp.int32)[None]
    row_index = row_index.reshape(1, WIDE)
    lo = jnp.where(row_index >= split, split, 0)

    own, other = [unit], [swap(unit)]
    for _ in range(3):
        own.append(along_z(own[-1]))
        other.append(along_z(other[-1]))
    own.append(along_z(own[-1]))

    mine = [unit] + [along_y(unit, dy) for dy in (1, -1, 2)]
    theirs = [other[0]] + [swap(segment) for segment in mine[1:]]

    def starts(pieces):
        return [start(0, toward * k, dcore) for k, dcore in pieces]

    right, best = match(
        first_kernel,
        starts([(0, 0), (1, 0), (1, 1)]),
        lo,
        row_index,
        mine + theirs,
        [unit, own[1], other[1]],
    )
    for k in (2, 3):
        best = match(
            match_kernel, starts([(k, 0), (k, 1)]), lo, row_index, [best, right], [own[k], other[k]]
        )
    best = match(match_kernel, starts([(4, 0)]), lo, row_index, [best, right], [own[4]])

    best = jnp.max(best, axis=0).reshape(CORES, Y, ROWS)
    best = jnp.maximum(best[0], swap(best[1]))
    best = jnp.maximum(
        jnp.maximum(best[0], along_y(best[1], -1)),
        jnp.maximum(along_y(best[2], 1), along_y(best[3], 2)),
    )
    return jnp.maximum(best, -1.0)


def solution(mesh):
    placed = (P(("group", "member"), None), P("group"))
    return jax.shard_map(
        shards, mesh=mesh, in_specs=placed, out_specs=P(("group", "member")), check_vma=False
    )
```

```python
import functools

import jax
import jax.numpy as jnp
from jax import lax
from jax.experimental import pallas as pl
from jax.experimental.pallas import tpu as pltpu
from jax.sharding import PartitionSpec as P

Y, Z, CORES = 4, 8, 2
ROWS = 192
SEGMENTS = Y * CORES
WIDE = SEGMENTS * ROWS
TILE = 256
D = 1024
NONE = -2.0
VMEM = pl.BlockSpec(memory_space=pltpu.VMEM)
SMEM = pl.BlockSpec(memory_space=pltpu.SMEM)


def device(y, z, core):
    return ((y % Y) * Z + z % Z) * CORES + core % CORES


def permute(value, target):
    pairs = [
        (device(y, z, core), device(*target(y, z, core)))
        for y in range(Y)
        for z in range(Z)
        for core in range(CORES)
    ]
    return lax.ppermute(value, "member", pairs)


def along_y(value, dy):
    return permute(value, lambda y, z, core: (y + (dy, -dy)[core], z, core))


def along_z(value):
    return permute(value, lambda y, z, core: (y, z + (1, -1)[core], core))


def swap(value):
    return permute(value, lambda y, z, core: (y, z, core + 1))


def normalize_kernel(rows_ref, unit_ref):
    values = rows_ref[...].astype(jnp.float32)
    unit_ref[...] = (
        values * lax.rsqrt(jnp.sum(values * values, axis=1, keepdims=True) + 1e-06)
    ).astype(jnp.bfloat16)


def normalize(rows):
    return pl.pallas_call(
        normalize_kernel,
        out_shape=jax.ShapeDtypeStruct((ROWS, D), jnp.bfloat16),
        in_specs=[VMEM],
        out_specs=VMEM,
        cost_estimate=pl.CostEstimate(flops=4 * ROWS * D, bytes_accessed=4 * ROWS * D, transcendentals=ROWS),
        compiler_params=pltpu.CompilerParams(vmem_limit_bytes=8 * 1024 * 1024),
        name="normalize",
    )(rows)


def fold(starts_ref, lo_ref, hi_ref, best_ref, right_ref, left, out_ref):
    for n in range(WIDE // TILE):
        lanes = slice(n * TILE, (n + 1) * TILE)
        scores = lax.dot_general(
            left[...], right_ref[lanes, :], (((1,), (1,)), ((), ())), preferred_element_type=jnp.float32
        )
        lo, hi = lo_ref[:, lanes], hi_ref[:, lanes]
        best = None if best_ref is None else best_ref[:, lanes]
        for i in range(left.shape[0] // ROWS):
            index = starts_ref[i] + lax.broadcasted_iota(jnp.int32, (ROWS, TILE), 0)
            part = jnp.where((index >= lo) & (index < hi), scores[i * ROWS : (i + 1) * ROWS], NONE)
            part = jnp.max(part.reshape(-1, 8, TILE), axis=0)
            best = part if best is None else jnp.maximum(best, part)
        out_ref[:, lanes] = best


def gather(piece_refs, left):
    first = 0
    for piece_ref in piece_refs:
        last = first + piece_ref.shape[0]
        left[first:last, :] = piece_ref[...]
        first = last
    return left


def first_kernel(starts_ref, lo_ref, hi_ref, *refs):
    segments, pieces = refs[:SEGMENTS], refs[SEGMENTS:-3]
    right_ref, out_ref, left = refs[-3:]
    gather(segments, right_ref)
    fold(starts_ref, lo_ref, hi_ref, None, right_ref, gather(pieces, left), out_ref)


def match_kernel(starts_ref, lo_ref, hi_ref, best_ref, right_ref, *refs):
    pieces, (out_ref, left) = refs[:-2], refs[-2:]
    fold(starts_ref, lo_ref, hi_ref, best_ref, right_ref, gather(pieces, left), out_ref)


def last_kernel(starts_ref, lo_ref, hi_ref, best_ref, right_ref, piece_ref, mine_ref, theirs_ref, best):
    fold(starts_ref, lo_ref, hi_ref, best_ref, right_ref, piece_ref, best)
    half = WIDE // CORES
    mine_ref[...] = jnp.max(best[:, :half], axis=0, keepdims=True)
    theirs_ref[...] = jnp.max(best[:, half:], axis=0, keepdims=True)


def match(kernel, starts, lo, hi, others, pieces):
    rows = ROWS * len(pieces)
    best = jax.ShapeDtypeStruct((8, WIDE), jnp.float32)
    out = best
    scratch = pltpu.VMEM((rows, D), jnp.bfloat16)
    if kernel is first_kernel:
        out = (jax.ShapeDtypeStruct((WIDE, D), jnp.bfloat16), best)
    if kernel is last_kernel:
        out = (jax.ShapeDtypeStruct((1, WIDE // CORES), jnp.float32),) * CORES
        scratch = pltpu.VMEM((8, WIDE), jnp.float32)
    return pl.pallas_call(
        kernel,
        out_shape=out,
        in_specs=[SMEM] + [VMEM] * (2 + len(others) + len(pieces)),
        out_specs=jax.tree.map(lambda _: VMEM, out),
        scratch_shapes=[scratch],
        cost_estimate=pl.CostEstimate(
            flops=2 * rows * WIDE * D, bytes_accessed=2 * D * (rows + WIDE), transcendentals=0
        ),
        compiler_params=pltpu.CompilerParams(vmem_limit_bytes=16 * 1024 * 1024),
        name="match",
    )(jnp.stack(starts), lo, hi, *others, *pieces)


def shards(embeddings, first_size):
    member = lax.axis_index("member")
    core = member % CORES
    z = member // CORES % Z
    y = member // (CORES * Z)
    split = first_size[0]
    toward = 2 * core - 1

    unit = normalize(embeddings)

    def start(dy, dz, dcore):
        return device(y + dy, z + dz, core + dcore) * ROWS

    row_index = jnp.concatenate(
        [
            start(toward * dy, 0, dcore) + jnp.arange(ROWS, dtype=jnp.int32)
            for dy, dcore in ((0, 0), (1, 0), (-1, 0), (2, 0), (0, 1), (-1, 1), (1, 1), (2, 1))
        ]
    )[None]
    lo = jnp.where(row_index >= split, split, 0)

    def after(value, *earlier):
        return lax.optimization_barrier((value,) + earlier)[0]

    partner = swap(unit)
    own, other = [unit], [partner]
    for _ in range(3):
        own.append(along_z(own[-1]))
        other.append(along_z(other[-1]))
    own.append(along_z(own[-1]))

    near = along_y(after(unit, partner), 1)
    near_other = along_y(after(partner, near), 1)
    far = along_y(near, 1)
    mine = [unit, near, swap(near_other), far]
    theirs = [partner, swap(near), near_other, swap(far)]

    def starts(pieces):
        return [start(0, toward * k, dcore) for k, dcore in pieces]

    right, best = match(
        first_kernel,
        starts([(0, 0), (1, 0), (1, 1)]),
        lo,
        row_index,
        mine + theirs,
        [unit, own[1], other[1]],
    )
    for k in (2, 3):
        best = match(
            match_kernel, starts([(k, 0), (k, 1)]), lo, row_index, [best, right], [own[k], other[k]]
        )
    mine, other = match(last_kernel, starts([(4, 0)]), lo, row_index, [best, right], [own[4]])

    best = jnp.maximum(mine, swap(other)).reshape(Y, ROWS)
    best = jnp.maximum(
        jnp.maximum(best[0], along_y(best[1], -1)),
        jnp.maximum(along_y(best[2], 1), along_y(best[3], 2)),
    )
    return jnp.maximum(best, -1.0)


def solution(mesh):
    placed = (P(("group", "member"), None), P("group"))
    return jax.shard_map(
        shards, mesh=mesh, in_specs=placed, out_specs=P(("group", "member")), check_vma=False
    )
```

```python
import functools

import jax
import jax.numpy as jnp
from jax import lax
from jax.experimental import pallas as pl
from jax.experimental.pallas import tpu as pltpu
from jax.sharding import PartitionSpec as P

Y, Z, CORES = 4, 8, 2
ROWS = 192
SEGMENTS = Y * CORES
WIDE = SEGMENTS * ROWS
HALF = WIDE // CORES
TILE = 256
D = 1024
NONE = -2.0
NEVER = 1 << 30
PIECES = ((0, 0), (1, 0), (1, 1), (2, 0), (2, 1), (3, 0), (3, 1), (4, 0))
VMEM = pl.BlockSpec(memory_space=pltpu.VMEM)
LAYOUT = ((0, 0), (1, 0), (-1, 0), (2, 0), (0, 1), (-1, 1), (1, 1), (2, 1))


def device(y, z, core):
    return ((y % Y) * Z + z % Z) * CORES + core % CORES


def permute(value, target):
    pairs = [
        (device(y, z, core), device(*target(y, z, core)))
        for y in range(Y)
        for z in range(Z)
        for core in range(CORES)
    ]
    return lax.ppermute(value, "member", pairs)


def along_y(value, dy):
    return permute(value, lambda y, z, core: (y + (dy, -dy)[core], z, core))


def along_z(value):
    return permute(value, lambda y, z, core: (y, z + (1, -1)[core], core))


def swap(value):
    return permute(value, lambda y, z, core: (y, z, core + 1))


def after(value, *earlier):
    return lax.optimization_barrier((value,) + earlier)[0]


def local(kernel, out_shape, operands, scratch=(), flops=0, mib=8, name=None):
    arrays = operands + jax.tree.leaves(out_shape)
    return pl.pallas_call(
        kernel,
        out_shape=out_shape,
        in_specs=[VMEM] * len(operands),
        out_specs=jax.tree.map(lambda _: VMEM, out_shape),
        scratch_shapes=list(scratch),
        cost_estimate=pl.CostEstimate(
            flops=flops,
            bytes_accessed=sum(array.size * array.dtype.itemsize for array in arrays),
            transcendentals=0,
        ),
        compiler_params=pltpu.CompilerParams(vmem_limit_bytes=mib * 1024 * 1024),
        name=name,
    )(*operands)


def normalize_kernel(rows_ref, unit_ref):
    values = rows_ref[...].astype(jnp.float32)
    unit_ref[...] = (
        values * lax.rsqrt(jnp.sum(values * values, axis=1, keepdims=True) + 1e-06)
    ).astype(jnp.bfloat16)


def normalize(rows):
    return local(normalize_kernel, jax.ShapeDtypeStruct(rows.shape, rows.dtype), [rows], name="normalize")


def first_rows(member, offsets, shape, axis):
    core = member % CORES
    z = member // CORES % Z
    y = member // (CORES * Z)
    toward = 1 - 2 * core
    slot = lax.broadcasted_iota(jnp.int32, shape, axis)
    rows = jnp.zeros(shape, jnp.int32)
    for i, (dy, dz, dcore) in enumerate(offsets):
        first = device(y - toward * dy, z - toward * dz, core + dcore) * ROWS
        if axis == len(shape) - 1:
            rows = jnp.where(slot >= i * ROWS, first + slot - i * ROWS, rows)
        else:
            rows = jnp.where(slot == i, first, rows)
    return rows


def gather(piece_refs, out_ref):
    for i, piece_ref in enumerate(piece_refs):
        out_ref[i * ROWS : (i + 1) * ROWS, :] = piece_ref[...]
    return out_ref


def fold(pieces, low_ref, high_ref, best_ref, right_ref, left, out_ref, first=0):
    for n in range(out_ref.shape[1] // TILE):
        lanes = slice(first + n * TILE, first + (n + 1) * TILE)
        scores = lax.dot_general(
            left[...], right_ref[lanes, :], (((1,), (1,)), ((), ())), preferred_element_type=jnp.float32
        )
        best = None if best_ref is None else best_ref[:, lanes]
        index = lax.broadcasted_iota(jnp.int32, (ROWS, TILE), 0)
        for i, piece in enumerate(pieces):
            keep = index >= low_ref[piece : piece + 1, lanes]
            if piece == 0:
                keep &= index < high_ref[:, lanes]
            part = jnp.where(keep, scores[i * ROWS : (i + 1) * ROWS], NONE)
            part = jnp.max(part.reshape(-1, 8, TILE), axis=0)
            best = part if best is None else jnp.maximum(best, part)
        out_ref[:, n * TILE : (n + 1) * TILE] = best


def first_kernel(pieces, low_ref, high_ref, *refs):
    segments, piece_refs = refs[:SEGMENTS], refs[SEGMENTS:-3]
    right_ref, out_ref, left = refs[-3:]
    gather(segments, right_ref)
    fold(pieces, low_ref, high_ref, None, right_ref, gather(piece_refs, left), out_ref)


def match_kernel(pieces, low_ref, best_ref, right_ref, *refs):
    *piece_refs, out_ref, left = refs
    fold(pieces, low_ref, None, best_ref, right_ref, gather(piece_refs, left), out_ref)


def last_kernel(first, pieces, low_ref, best_ref, right_ref, piece_ref, out_ref, best):
    fold(pieces, low_ref, None, best_ref, right_ref, piece_ref, best, first)
    out_ref[...] = jnp.max(best[...], axis=0, keepdims=True)


def match(kernel, pieces, operands):
    rows = ROWS * len(pieces)
    best = jax.ShapeDtypeStruct((8, WIDE), jnp.float32)
    out, scratch = best, pltpu.VMEM((rows, D), jnp.bfloat16)
    if kernel is first_kernel:
        out = (jax.ShapeDtypeStruct((WIDE, D), jnp.bfloat16), best)
    return local(
        functools.partial(kernel, pieces),
        out,
        operands,
        scratch=[scratch],
        flops=2 * rows * WIDE * D,
        mib=16,
        name="match",
    )


def last(first, pieces, operands):
    return local(
        functools.partial(last_kernel, first, pieces),
        jax.ShapeDtypeStruct((1, HALF), jnp.float32),
        operands,
        scratch=[pltpu.VMEM((8, HALF), jnp.float32)],
        flops=2 * ROWS * HALF * D,
        mib=16,
        name="last",
    )


def shards(embeddings, first_size):
    member = lax.axis_index("member")
    split = first_size[0]
    row = first_rows(member, [(dy, 0, dcore) for dy, dcore in LAYOUT], (1, WIDE), 1)
    start = first_rows(member, [(0, dz, dcore) for dz, dcore in PIECES], (len(PIECES), WIDE), 0)
    low = jnp.where(row > start, jnp.where(row >= split, split, 0) - start, NEVER)
    high = row - start[:1]

    unit = normalize(embeddings)
    own = [unit, along_z(unit)]
    partner = swap(unit)
    other = [partner, along_z(partner)]
    for k in (1, 2):
        own.append(along_z(own[k]))
        other.append(along_z(other[k]))
    own.append(along_z(own[3]))

    near = along_y(after(unit, partner), 1)
    near_other = along_y(after(partner, near), 1)
    far = along_y(near, 1)
    mine = [unit, near, swap(after(near_other, own[2])), far]
    theirs = [partner, swap(after(near, other[1])), near_other, swap(after(far, other[2]))]

    right, best = match(first_kernel, (0, 1, 2), [low, high, *mine, *theirs, unit, own[1], other[1]])
    best = match(match_kernel, (3, 4), [low, best, right, own[2], other[2]])
    best = match(match_kernel, (5, 6), [low, best, right, own[3], other[3]])
    others = swap(last(HALF, (7,), [low, best, right, own[4]]))
    best = last(0, (7,), [low, best, right, own[4]])

    best = jnp.maximum(best, others).reshape(Y, ROWS)
    far_best = along_y(best[3], 2)
    best = jnp.maximum(
        jnp.maximum(best[0], far_best), jnp.maximum(along_y(best[2], 1), along_y(best[1], -1))
    )
    return jnp.maximum(best, -1.0)


def solution(mesh):
    placed = (P(("group", "member"), None), P("group"))
    return jax.shard_map(
        shards, mesh=mesh, in_specs=placed, out_specs=P(("group", "member")), check_vma=False
    )
```

```python
import functools

import jax
import jax.numpy as jnp
from jax import lax
from jax.experimental import pallas as pl
from jax.experimental.pallas import tpu as pltpu
from jax.sharding import PartitionSpec as P

Y, Z, CORES = 4, 8, 2
ROWS = 192
SEGMENTS = Y * CORES
WIDE = SEGMENTS * ROWS
HALF = WIDE // CORES
TILE = 256
D = 1024
NONE = -2.0
NEVER = 1 << 30
PIECES = ((0, 0), (1, 0), (1, 1), (2, 0), (2, 1), (3, 0), (3, 1), (4, 0))
VMEM = pl.BlockSpec(memory_space=pltpu.VMEM)
LAYOUT = ((0, 0), (1, 0), (-1, 0), (2, 0), (0, 1), (-1, 1), (1, 1), (2, 1))


def device(y, z, core):
    return ((y % Y) * Z + z % Z) * CORES + core % CORES


def permute(value, target):
    pairs = [
        (device(y, z, core), device(*target(y, z, core)))
        for y in range(Y)
        for z in range(Z)
        for core in range(CORES)
    ]
    return lax.ppermute(value, "member", pairs)


def along_y(value, dy):
    return permute(value, lambda y, z, core: (y + (dy, -dy)[core], z, core))


def along_z(value):
    return permute(value, lambda y, z, core: (y, z + (1, -1)[core], core))


def swap(value):
    return permute(value, lambda y, z, core: (y, z, core + 1))


def after(value, *earlier):
    return lax.optimization_barrier((value,) + earlier)[0]


def local(kernel, out_shape, operands, scratch=(), flops=0, mib=8, name=None):
    arrays = operands + jax.tree.leaves(out_shape)
    return pl.pallas_call(
        kernel,
        out_shape=out_shape,
        in_specs=[VMEM] * len(operands),
        out_specs=jax.tree.map(lambda _: VMEM, out_shape),
        scratch_shapes=list(scratch),
        cost_estimate=pl.CostEstimate(
            flops=flops,
            bytes_accessed=sum(array.size * array.dtype.itemsize for array in arrays),
            transcendentals=0,
        ),
        compiler_params=pltpu.CompilerParams(vmem_limit_bytes=mib * 1024 * 1024),
        name=name,
    )(*operands)


def normalize_kernel(rows_ref, unit_ref):
    values = rows_ref[...].astype(jnp.float32)
    unit_ref[...] = (
        values * lax.rsqrt(jnp.sum(values * values, axis=1, keepdims=True) + 1e-06)
    ).astype(jnp.bfloat16)


def normalize(rows):
    return local(normalize_kernel, jax.ShapeDtypeStruct(rows.shape, rows.dtype), [rows], name="normalize")


def first_rows(member, offsets, shape, axis):
    core = member % CORES
    z = member // CORES % Z
    y = member // (CORES * Z)
    toward = 1 - 2 * core
    slot = lax.broadcasted_iota(jnp.int32, shape, axis)
    rows = jnp.zeros(shape, jnp.int32)
    for i, (dy, dz, dcore) in enumerate(offsets):
        first = device(y - toward * dy, z - toward * dz, core + dcore) * ROWS
        if axis == len(shape) - 1:
            rows = jnp.where(slot >= i * ROWS, first + slot - i * ROWS, rows)
        else:
            rows = jnp.where(slot == i, first, rows)
    return rows


def gather(piece_refs, out_ref):
    for i, piece_ref in enumerate(piece_refs):
        out_ref[i * ROWS : (i + 1) * ROWS, :] = piece_ref[...]
    return out_ref


def fold(pieces, low_ref, high_ref, best_ref, right_ref, left, out_ref, first=0):
    for n in range(out_ref.shape[1] // TILE):
        lanes = slice(first + n * TILE, first + (n + 1) * TILE)
        scores = lax.dot_general(
            left[...], right_ref[lanes, :], (((1,), (1,)), ((), ())), preferred_element_type=jnp.float32
        )
        best = None if best_ref is None else best_ref[:, lanes]
        index = lax.broadcasted_iota(jnp.int32, (ROWS, TILE), 0)
        for i, piece in enumerate(pieces):
            keep = index >= low_ref[piece : piece + 1, lanes]
            if piece == 0:
                keep &= index < high_ref[:, lanes]
            part = jnp.where(keep, scores[i * ROWS : (i + 1) * ROWS], NONE)
            part = jnp.max(part.reshape(-1, 8, TILE), axis=0)
            best = part if best is None else jnp.maximum(best, part)
        out_ref[:, n * TILE : (n + 1) * TILE] = best


def first_kernel(pieces, low_ref, high_ref, *refs):
    segments, piece_refs = refs[:SEGMENTS], refs[SEGMENTS:-3]
    right_ref, out_ref, left = refs[-3:]
    gather(segments, right_ref)
    fold(pieces, low_ref, high_ref, None, right_ref, gather(piece_refs, left), out_ref)


def match_kernel(pieces, low_ref, best_ref, right_ref, *refs):
    *piece_refs, out_ref, left = refs
    fold(pieces, low_ref, None, best_ref, right_ref, gather(piece_refs, left), out_ref)


def last_kernel(first, pieces, low_ref, best_ref, right_ref, piece_ref, out_ref, best):
    fold(pieces, low_ref, None, best_ref, right_ref, piece_ref, best, first)
    out_ref[...] = jnp.max(best[...], axis=0, keepdims=True)


def match(kernel, pieces, operands):
    rows = ROWS * len(pieces)
    best = jax.ShapeDtypeStruct((8, WIDE), jnp.float32)
    out, scratch = best, pltpu.VMEM((rows, D), jnp.bfloat16)
    if kernel is first_kernel:
        out = (jax.ShapeDtypeStruct((WIDE, D), jnp.bfloat16), best)
    return local(
        functools.partial(kernel, pieces),
        out,
        operands,
        scratch=[scratch],
        flops=2 * rows * WIDE * D,
        mib=16,
        name="match",
    )


def last(first, pieces, operands):
    return local(
        functools.partial(last_kernel, first, pieces),
        jax.ShapeDtypeStruct((1, HALF), jnp.float32),
        operands,
        scratch=[pltpu.VMEM((8, HALF), jnp.float32)],
        flops=2 * ROWS * HALF * D,
        mib=16,
        name="last",
    )


def shards(embeddings, first_size):
    member = lax.axis_index("member")
    split = first_size[0]
    row = first_rows(member, [(dy, 0, dcore) for dy, dcore in LAYOUT], (1, WIDE), 1)
    start = first_rows(member, [(0, dz, dcore) for dz, dcore in PIECES], (len(PIECES), WIDE), 0)
    low = jnp.where(row > start, jnp.where(row >= split, split, 0) - start, NEVER)
    high = row - start[:1]

    unit = normalize(embeddings)
    own = [unit, along_z(unit)]
    partner = swap(unit)
    other = [partner, along_z(partner)]
    for k in (1, 2):
        own.append(along_z(own[k]))
        other.append(along_z(other[k]))
    own.append(along_z(own[3]))

    near = along_y(after(unit, partner), 1)
    near_other = along_y(partner, 1)
    far = along_y(near, 1)
    mine = [unit, near, swap(near_other), far]
    theirs = [partner, swap(after(near, other[1])), near_other, swap(far)]

    right, best = match(first_kernel, (0, 1, 2), [low, high, *mine, *theirs, unit, own[1], other[1]])
    best = match(match_kernel, (3, 4), [low, best, right, own[2], other[2]])
    best = match(match_kernel, (5, 6), [low, best, right, own[3], other[3]])
    others = swap(last(HALF, (7,), [low, best, right, own[4]]))
    best = last(0, (7,), [low, best, right, own[4]])

    best = jnp.maximum(best, others).reshape(Y, ROWS)
    far_best = along_y(best[3], 2)
    best = jnp.maximum(
        jnp.maximum(best[0], far_best), jnp.maximum(along_y(best[2], 1), along_y(best[1], -1))
    )
    return jnp.maximum(best, -1.0)


def solution(mesh):
    placed = (P(("group", "member"), None), P("group"))
    return jax.shard_map(
        shards, mesh=mesh, in_specs=placed, out_specs=P(("group", "member")), check_vma=False
    )
```

```python
import functools

import jax
import jax.numpy as jnp
from jax import lax
from jax.experimental import pallas as pl
from jax.experimental.pallas import tpu as pltpu
from jax.sharding import PartitionSpec as P

Y, Z, CORES = 4, 8, 2
ROWS = 192
SEGMENTS = Y * CORES
WIDE = SEGMENTS * ROWS
HALF = WIDE // CORES
TILE = 256
D = 1024
NONE = -2.0
NEVER = 1 << 30
PIECES = ((0, 0), (1, 0), (1, 1), (2, 0), (2, 1), (3, 0), (3, 1), (4, 0))
VMEM = pl.BlockSpec(memory_space=pltpu.VMEM)
LAYOUT = ((0, 0), (1, 0), (-1, 0), (2, 0), (0, 1), (-1, 1), (1, 1), (2, 1))


def device(y, z, core):
    return ((y % Y) * Z + z % Z) * CORES + core % CORES


def permute(value, target):
    pairs = [
        (device(y, z, core), device(*target(y, z, core)))
        for y in range(Y)
        for z in range(Z)
        for core in range(CORES)
    ]
    return lax.ppermute(value, "member", pairs)


def along_y(value, dy):
    return permute(value, lambda y, z, core: (y + (dy, -dy)[core], z, core))


def along_z(value):
    return permute(value, lambda y, z, core: (y, z + (1, -1)[core], core))


def swap(value):
    return permute(value, lambda y, z, core: (y, z, core + 1))


def after(value, *earlier):
    return lax.optimization_barrier((value,) + earlier)[0]


def local(kernel, out_shape, operands, scratch=(), flops=0, mib=8, name=None):
    arrays = operands + jax.tree.leaves(out_shape)
    return pl.pallas_call(
        kernel,
        out_shape=out_shape,
        in_specs=[VMEM] * len(operands),
        out_specs=jax.tree.map(lambda _: VMEM, out_shape),
        scratch_shapes=list(scratch),
        cost_estimate=pl.CostEstimate(
            flops=flops,
            bytes_accessed=sum(array.size * array.dtype.itemsize for array in arrays),
            transcendentals=0,
        ),
        compiler_params=pltpu.CompilerParams(vmem_limit_bytes=mib * 1024 * 1024),
        name=name,
    )(*operands)


def normalize_kernel(rows_ref, unit_ref):
    values = rows_ref[...].astype(jnp.float32)
    unit_ref[...] = (
        values * lax.rsqrt(jnp.sum(values * values, axis=1, keepdims=True) + 1e-06)
    ).astype(jnp.bfloat16)


def normalize(rows):
    return local(normalize_kernel, jax.ShapeDtypeStruct(rows.shape, rows.dtype), [rows], name="normalize")


def first_rows(member, offsets, shape, axis):
    core = member % CORES
    z = member // CORES % Z
    y = member // (CORES * Z)
    toward = 1 - 2 * core
    slot = lax.broadcasted_iota(jnp.int32, shape, axis)
    rows = jnp.zeros(shape, jnp.int32)
    for i, (dy, dz, dcore) in enumerate(offsets):
        first = device(y - toward * dy, z - toward * dz, core + dcore) * ROWS
        if axis == len(shape) - 1:
            rows = jnp.where(slot >= i * ROWS, first + slot - i * ROWS, rows)
        else:
            rows = jnp.where(slot == i, first, rows)
    return rows


def gather(piece_refs, out_ref):
    for i, piece_ref in enumerate(piece_refs):
        out_ref[i * ROWS : (i + 1) * ROWS, :] = piece_ref[...]
    return out_ref


def fold(pieces, low_ref, high_ref, best_ref, right_ref, left, out_ref, first=0):
    for n in range(out_ref.shape[1] // TILE):
        lanes = slice(first + n * TILE, first + (n + 1) * TILE)
        scores = lax.dot_general(
            left[...], right_ref[lanes, :], (((1,), (1,)), ((), ())), preferred_element_type=jnp.float32
        )
        best = None if best_ref is None else best_ref[:, lanes]
        index = lax.broadcasted_iota(jnp.int32, (ROWS, TILE), 0)
        for i, piece in enumerate(pieces):
            keep = index >= low_ref[piece : piece + 1, lanes]
            if piece == 0:
                keep &= index < high_ref[:, lanes]
            part = jnp.where(keep, scores[i * ROWS : (i + 1) * ROWS], NONE)
            part = jnp.max(part.reshape(-1, 8, TILE), axis=0)
            best = part if best is None else jnp.maximum(best, part)
        out_ref[:, n * TILE : (n + 1) * TILE] = best


def first_kernel(pieces, low_ref, high_ref, *refs):
    segments, piece_refs = refs[:SEGMENTS], refs[SEGMENTS:-3]
    right_ref, out_ref, left = refs[-3:]
    gather(segments, right_ref)
    fold(pieces, low_ref, high_ref, None, right_ref, gather(piece_refs, left), out_ref)


def match_kernel(pieces, low_ref, best_ref, right_ref, *refs):
    *piece_refs, out_ref, left = refs
    fold(pieces, low_ref, None, best_ref, right_ref, gather(piece_refs, left), out_ref)


def last_kernel(first, pieces, low_ref, best_ref, right_ref, piece_ref, out_ref, best):
    fold(pieces, low_ref, None, best_ref, right_ref, piece_ref, best, first)
    out_ref[...] = jnp.max(best[...], axis=0, keepdims=True)


def match(kernel, pieces, operands):
    rows = ROWS * len(pieces)
    best = jax.ShapeDtypeStruct((8, WIDE), jnp.float32)
    out, scratch = best, pltpu.VMEM((rows, D), jnp.bfloat16)
    if kernel is first_kernel:
        out = (jax.ShapeDtypeStruct((WIDE, D), jnp.bfloat16), best)
    return local(
        functools.partial(kernel, pieces),
        out,
        operands,
        scratch=[scratch],
        flops=2 * rows * WIDE * D,
        mib=16,
        name="match",
    )


def last(first, pieces, operands):
    return local(
        functools.partial(last_kernel, first, pieces),
        jax.ShapeDtypeStruct((1, HALF), jnp.float32),
        operands,
        scratch=[pltpu.VMEM((8, HALF), jnp.float32)],
        flops=2 * ROWS * HALF * D,
        mib=16,
        name="last",
    )


def shards(embeddings, first_size):
    member = lax.axis_index("member")
    split = first_size[0]
    row = first_rows(member, [(dy, 0, dcore) for dy, dcore in LAYOUT], (1, WIDE), 1)
    start = first_rows(member, [(0, dz, dcore) for dz, dcore in PIECES], (len(PIECES), WIDE), 0)
    low = jnp.where(row > start, jnp.where(row >= split, split, 0) - start, NEVER)
    high = row - start[:1]

    unit = normalize(embeddings)
    own = [unit, along_z(unit)]
    partner = swap(unit)
    other = [partner, along_z(partner)]
    for k in (1, 2):
        own.append(along_z(own[k]))
        other.append(along_z(other[k]))
    own.append(along_z(own[3]))

    near = along_y(after(unit, partner), 1)
    near_other = along_y(partner, 1)
    far = along_y(near, 1)
    mine = [unit, near, swap(near_other), far]
    theirs = [partner, swap(near), near_other, swap(far)]

    right, best = match(first_kernel, (0, 1, 2), [low, high, *mine, *theirs, unit, own[1], other[1]])
    best = match(match_kernel, (3, 4), [low, best, right, own[2], other[2]])
    best = match(match_kernel, (5, 6), [low, best, right, own[3], other[3]])
    others = swap(last(HALF, (7,), [low, best, right, own[4]]))
    best = last(0, (7,), [low, best, right, own[4]])

    best = jnp.maximum(best, others).reshape(Y, ROWS)
    far_best = along_y(best[3], 2)
    best = jnp.maximum(
        jnp.maximum(best[0], far_best), jnp.maximum(along_y(best[2], 1), along_y(best[1], -1))
    )
    return jnp.maximum(best, -1.0)


def solution(mesh):
    placed = (P(("group", "member"), None), P("group"))
    return jax.shard_map(
        shards, mesh=mesh, in_specs=placed, out_specs=P(("group", "member")), check_vma=False
    )
```

```python
import functools

import jax
import jax.numpy as jnp
from jax import lax
from jax.experimental import pallas as pl
from jax.experimental.pallas import tpu as pltpu
from jax.sharding import PartitionSpec as P

Y, Z, CORES = 4, 8, 2
ROWS = 192
SEGMENTS = Y * CORES
WIDE = SEGMENTS * ROWS
HALF = WIDE // CORES
TILE = 256
D = 1024
NONE = -2.0
NEVER = 1 << 30
PIECES = ((0, 0), (1, 0), (1, 1), (2, 0), (2, 1), (3, 0), (3, 1), (4, 0))
VMEM = pl.BlockSpec(memory_space=pltpu.VMEM)
LAYOUT = ((0, 0), (1, 0), (-1, 0), (2, 0), (0, 1), (-1, 1), (1, 1), (2, 1))


def device(y, z, core):
    return ((y % Y) * Z + z % Z) * CORES + core % CORES


def permute(value, target):
    pairs = [
        (device(y, z, core), device(*target(y, z, core)))
        for y in range(Y)
        for z in range(Z)
        for core in range(CORES)
    ]
    return lax.ppermute(value, "member", pairs)


def along_y(value, dy):
    return permute(value, lambda y, z, core: (y + (dy, -dy)[core], z, core))


def along_z(value):
    return permute(value, lambda y, z, core: (y, z + (1, -1)[core], core))


def swap(value):
    return permute(value, lambda y, z, core: (y, z, core + 1))


def after(value, *earlier):
    return lax.optimization_barrier((value,) + earlier)[0]


def local(kernel, out_shape, operands, scratch=(), flops=0, mib=8, name=None):
    arrays = operands + jax.tree.leaves(out_shape)
    return pl.pallas_call(
        kernel,
        out_shape=out_shape,
        in_specs=[VMEM] * len(operands),
        out_specs=jax.tree.map(lambda _: VMEM, out_shape),
        scratch_shapes=list(scratch),
        cost_estimate=pl.CostEstimate(
            flops=flops,
            bytes_accessed=sum(array.size * array.dtype.itemsize for array in arrays),
            transcendentals=0,
        ),
        compiler_params=pltpu.CompilerParams(vmem_limit_bytes=mib * 1024 * 1024),
        name=name,
    )(*operands)


def normalize_kernel(rows_ref, unit_ref):
    values = rows_ref[...].astype(jnp.float32)
    unit_ref[...] = (
        values * lax.rsqrt(jnp.sum(values * values, axis=1, keepdims=True) + 1e-06)
    ).astype(jnp.bfloat16)


def normalize(rows):
    return local(normalize_kernel, jax.ShapeDtypeStruct(rows.shape, rows.dtype), [rows], name="normalize")


def first_rows(member, offsets, shape, axis):
    core = member % CORES
    z = member // CORES % Z
    y = member // (CORES * Z)
    toward = 1 - 2 * core
    slot = lax.broadcasted_iota(jnp.int32, shape, axis)
    rows = jnp.zeros(shape, jnp.int32)
    for i, (dy, dz, dcore) in enumerate(offsets):
        first = device(y - toward * dy, z - toward * dz, core + dcore) * ROWS
        if axis == len(shape) - 1:
            rows = jnp.where(slot >= i * ROWS, first + slot - i * ROWS, rows)
        else:
            rows = jnp.where(slot == i, first, rows)
    return rows


def gather(piece_refs, out_ref):
    for i, piece_ref in enumerate(piece_refs):
        out_ref[i * ROWS : (i + 1) * ROWS, :] = piece_ref[...]
    return out_ref


def fold(pieces, low_ref, high_ref, best_ref, right_ref, left, out_ref, first=0):
    for n in range(out_ref.shape[1] // TILE):
        lanes = slice(first + n * TILE, first + (n + 1) * TILE)
        scores = lax.dot_general(
            left[...], right_ref[lanes, :], (((1,), (1,)), ((), ())), preferred_element_type=jnp.float32
        )
        best = None if best_ref is None else best_ref[:, lanes]
        index = lax.broadcasted_iota(jnp.int32, (ROWS, TILE), 0)
        for i, piece in enumerate(pieces):
            keep = index >= low_ref[piece : piece + 1, lanes]
            if piece == 0:
                keep &= index < high_ref[:, lanes]
            part = jnp.where(keep, scores[i * ROWS : (i + 1) * ROWS], NONE)
            part = jnp.max(part.reshape(-1, 8, TILE), axis=0)
            best = part if best is None else jnp.maximum(best, part)
        out_ref[:, n * TILE : (n + 1) * TILE] = best


def first_kernel(pieces, low_ref, high_ref, *refs):
    segments, piece_refs = refs[:SEGMENTS], refs[SEGMENTS:-3]
    right_ref, out_ref, left = refs[-3:]
    gather(segments, right_ref)
    fold(pieces, low_ref, high_ref, None, right_ref, gather(piece_refs, left), out_ref)


def match_kernel(pieces, low_ref, best_ref, right_ref, *refs):
    *piece_refs, out_ref, left = refs
    fold(pieces, low_ref, None, best_ref, right_ref, gather(piece_refs, left), out_ref)


def last_kernel(first, pieces, low_ref, best_ref, right_ref, piece_ref, out_ref, best):
    fold(pieces, low_ref, None, best_ref, right_ref, piece_ref, best, first)
    out_ref[...] = jnp.max(best[...], axis=0, keepdims=True)


def match(kernel, pieces, operands):
    rows = ROWS * len(pieces)
    best = jax.ShapeDtypeStruct((8, WIDE), jnp.float32)
    out, scratch = best, pltpu.VMEM((rows, D), jnp.bfloat16)
    if kernel is first_kernel:
        out = (jax.ShapeDtypeStruct((WIDE, D), jnp.bfloat16), best)
    return local(
        functools.partial(kernel, pieces),
        out,
        operands,
        scratch=[scratch],
        flops=2 * rows * WIDE * D,
        mib=16,
        name="match",
    )


def last(first, pieces, operands):
    return local(
        functools.partial(last_kernel, first, pieces),
        jax.ShapeDtypeStruct((1, HALF), jnp.float32),
        operands,
        scratch=[pltpu.VMEM((8, HALF), jnp.float32)],
        flops=2 * ROWS * HALF * D,
        mib=16,
        name="last",
    )


def shards(embeddings, first_size):
    member = lax.axis_index("member")
    split = first_size[0]
    row = first_rows(member, [(dy, 0, dcore) for dy, dcore in LAYOUT], (1, WIDE), 1)
    start = first_rows(member, [(0, dz, dcore) for dz, dcore in PIECES], (len(PIECES), WIDE), 0)
    low = jnp.where(row > start, jnp.where(row >= split, split, 0) - start, NEVER)
    high = row - start[:1]

    unit = normalize(embeddings)
    own = [unit, along_z(unit)]
    partner = swap(unit)
    other = [partner, along_z(partner)]
    for k in (1, 2):
        own.append(along_z(own[k]))
        other.append(along_z(other[k]))
    own.append(along_z(own[3]))

    near = along_y(unit, 1)
    near_other = along_y(partner, 1)
    far = along_y(near, 1)
    mine = [unit, near, swap(near_other), far]
    theirs = [partner, swap(after(near, other[1])), near_other, swap(far)]

    right, best = match(first_kernel, (0, 1, 2), [low, high, *mine, *theirs, unit, own[1], other[1]])
    best = match(match_kernel, (3, 4), [low, best, right, own[2], other[2]])
    best = match(match_kernel, (5, 6), [low, best, right, own[3], other[3]])
    others = swap(last(HALF, (7,), [low, best, right, own[4]]))
    best = last(0, (7,), [low, best, right, own[4]])

    best = jnp.maximum(best, others).reshape(Y, ROWS)
    far_best = along_y(best[3], 2)
    best = jnp.maximum(
        jnp.maximum(best[0], far_best), jnp.maximum(along_y(best[2], 1), along_y(best[1], -1))
    )
    return jnp.maximum(best, -1.0)


def solution(mesh):
    placed = (P(("group", "member"), None), P("group"))
    return jax.shard_map(
        shards, mesh=mesh, in_specs=placed, out_specs=P(("group", "member")), check_vma=False
    )
```
